32 devices in a mesh: grid: 8 (over z, x), orb: 4 (over y, core).
Axes of the slice: x: 2, y: 2, z: 4, core: 2. Of those that a mesh axis runs over, the one named last changes fastest.
Arguments:
- collocation: bfloat16 [3072, 8192], P('orb', 'grid'), may hold values from -6 to 6
- amplitude: bfloat16 [3072, 1536], P('orb'), may hold values from -0.109375 to 0.109375
- occupied: bfloat16 [1536, 8192], P('orb', 'grid'), may hold values from -6 to 6
- quadrature: bfloat16 [8192, 1536], P('grid'), may hold values from -6 to 6
- pair_list: int32 [8, 4, 48], P('grid', 'orb'), may hold values from 0 to 47, as said below
- pair_count: int32 [8, 4], P('grid', 'orb'), may hold values from 12 to 48, as said below
Outputs:
- residual: float32 [1536, 3072], P('grid', 'orb')
The draws below stay inside these ranges and needn't reach their ends.
Inputs may be any that keep to these rules, and one draw needn't show every extreme that they name: `pair_list`: within each device's list the entries are distinct. `pair_count`: some device has all 48 pairs live.
All inputs are finite; a program needn't handle non-finite values.
Results may differ from the reference program's by a relative error of at most 0.0045.
Values may be sent and summed in bfloat16 or wider, within the bound.
A program may use at most 64 MiB of HBM per device.

```python
import math
import jax
import jax.numpy as jnp
from jax import lax

BLK = 128
OB_DEV = 6
GB_DEV = 8
R = 1536
NV = 3072
NG = 8192
N_GRID = 8
N_ORB = 4


def draw_pair_list(key, part):
    key = jax.random.fold_in(key, 11)
    slots = GB_DEV * OB_DEV
    keys = jax.random.split(key, N_GRID * N_ORB)
    orders = jax.vmap(lambda one: jax.random.permutation(one, slots))(keys)
    return orders.astype(jnp.int32).reshape(N_GRID, N_ORB, slots)


def draw_pair_count(key, part):
    key = jax.random.fold_in(key, 23)
    slots = GB_DEV * OB_DEV
    first, second = jax.random.split(key)
    counts = jax.random.randint(first, (N_GRID * N_ORB,), slots // 4, slots + 1)
    chosen = jax.random.randint(second, (), 0, N_GRID * N_ORB)
    counts = jnp.where(jnp.arange(N_GRID * N_ORB) == chosen, slots, counts)
    return counts.astype(jnp.int32).reshape(N_GRID, N_ORB)


def levels(key, extent, cuts, least, top_value):
    gain = 1.0
    for axis_at, parts in cuts:
        steps = jax.random.uniform(jax.random.fold_in(jax.random.fold_in(key, 6), axis_at), (parts,), jnp.float32, least / len(cuts), top_value / len(cuts))
        gain = gain * jnp.repeat(jnp.exp(steps), extent[axis_at] // parts).reshape((-1,) + (1,) * (len(extent) - 1 - axis_at))
    return gain


def gaussian(own_key, extent, scale, reach, cuts=(), kind=jnp.bfloat16):
    values = scale * jax.random.normal(own_key, extent, jnp.float32)
    if cuts:
        values = values * levels(own_key, extent, cuts, -0.22, 0.18)
    return jnp.clip(values, -reach, reach).astype(kind)


def setup_inputs(seed: int = 0) -> dict:
    seeds = jax.random.split(jax.random.key(seed), 7)
    return {
        "collocation": gaussian(seeds[0], (NV, NG), 1.0, 6.0, ((0, 4), (1, 8))),
        "amplitude": gaussian(seeds[1], (NV, R), NV ** -0.5, 0.109375, ((0, 4),)),
        "occupied": gaussian(seeds[2], (R, NG), 1.0, 6.0, ((0, 4), (1, 8))),
        "quadrature": gaussian(seeds[3], (NG, R), 1.0, 6.0, ((0, 8),)),
        "pair_list": draw_pair_list(jax.random.fold_in(seeds[6], 71), 0),
        "pair_count": draw_pair_count(jax.random.fold_in(seeds[6], 71), 0),
    }


def reference(collocation, amplitude, occupied, quadrature, pair_list, pair_count):
    slots = GB_DEV * OB_DEV
    orb_rows = OB_DEV * BLK
    grid_cols = GB_DEV * BLK
    numbers = jnp.arange(slots, dtype=jnp.int32)
    live = numbers[None, None, :] < pair_count[:, :, None]
    hits = jnp.logical_and(pair_list[:, :, :, None] == numbers[None, None, None, :], live[:, :, :, None])
    screen = jnp.any(hits, axis=2).astype(jnp.float32).reshape(N_GRID, N_ORB, GB_DEV, OB_DEV)
    factor = amplitude.astype(jnp.float32).reshape(N_ORB, orb_rows, R)

    def front(index):
        cols = lax.dynamic_slice_in_dim(collocation, index * grid_cols, grid_cols, 1).astype(jnp.float32)
        local_screen = jnp.transpose(screen[index], (0, 2, 1))
        block = cols.reshape(N_ORB, OB_DEV, BLK, GB_DEV, BLK) * local_screen[:, :, None, :, None]
        partial_sums = jnp.einsum('oar,oap->orp', factor, block.reshape(N_ORB, orb_rows, grid_cols))
        return lax.optimization_barrier(jnp.sum(partial_sums, axis=0))
    pieces = lax.map(front, jnp.arange(N_GRID, dtype=jnp.int32))
    projected = jnp.transpose(pieces, (1, 0, 2)).reshape(R, NG)
    hadamard = (projected * occupied.astype(jnp.float32)).astype(jnp.bfloat16)
    ladder = (jnp.dot(hadamard, quadrature, preferred_element_type=jnp.float32) * (1.0 / math.sqrt(NG))).astype(jnp.bfloat16)
    spread = lax.dot_general(ladder, quadrature, (((1,), (1,)), ((), ())), preferred_element_type=jnp.float32)
    back = (occupied.astype(jnp.float32) * spread * (1.0 / math.sqrt(R))).astype(jnp.bfloat16)
    total = lax.dot_general(back, collocation, (((1,), (1,)), ((), ())), preferred_element_type=jnp.float32)
    return total * (1.0 / math.sqrt(NG))
```

```python
import functools
import math

import jax
import jax.numpy as jnp
from jax import lax
from jax.experimental import pallas as pl
from jax.experimental.pallas import tpu as pltpu
from jax.sharding import PartitionSpec as P

BLK = 128
OB_DEV = 6
GB_DEV = 8
CORES = 2
UNIT = 48
MESH = pl.DeviceIdType.MESH
F32 = jnp.float32
BF16 = jnp.bfloat16


def kernel(
    n_grid, n_orb, n_x, chunks, total_grid,
    coll_ref, amp_ref, occ_ref, quad_ref, list_ref, count_ref, out_ref,
    masked, other1, own1, recv1, ysend, yrecv, had, lpart, lxsend, lxrecv, lzsend, lzrecv,
    ladder, ladder_flat, back, rpart, rxsend, rxrecv, rzsend, rzrecv,
    c1_s, c1_r, y1_s, y1_r, lx_s, lx_r, lz_s, lz_r, gz_s, gz_r, gx_s, gx_r,
    by_s, by_r, bc_s, bc_r, rx_s, rx_r, rz_s, rz_r,
):
    n_y = n_orb // CORES
    n_z = n_grid // n_x
    a_dev, pts = coll_ref.shape
    rank = quad_ref.shape[1]
    rows_orb = rank // n_orb
    rows_dev = rank // n_grid
    unit = rows_dev // chunks
    wide = n_x * unit
    cols = rank // n_z
    inv_grid = 1.0 / math.sqrt(total_grid)
    inv_rank = 1.0 / math.sqrt(rank)

    g, o = lax.axis_index("grid"), lax.axis_index("orb")
    z, x = g // n_x, g % n_x
    y, core = o // CORES, o % CORES

    core_peer = (g, y * CORES + (1 - core))
    ys = [(y + d) % n_y for d in range(1, n_y)]
    xs = [(x + d) % n_x for d in range(1, n_x)]
    zs = [(z + d) % n_z for d in range(1, n_z)]
    y_peers = [(g, q * CORES + core) for q in ys]
    x_peers = [(z * n_x + q, o) for q in xs]
    z_peers = [(q * n_x + x, o) for q in zs]

    barrier = pltpu.get_barrier_semaphore()
    peers = [core_peer] + y_peers + x_peers + z_peers
    for peer in peers:
        pl.semaphore_signal(barrier, inc=1, device_id=peer, device_id_type=MESH)

    def remote(src, dst, send, recv, peer):
        return pltpu.make_async_remote_copy(
            src_ref=src, dst_ref=dst, send_sem=send, recv_sem=recv, device_id=peer, device_id_type=MESH
        )

    def core_sum(c):
        return remote(other1.at[c], recv1.at[c], c1_s.at[c], c1_r.at[c], core_peer)

    def y_sum(c, d):
        return remote(ysend.at[c, d], yrecv.at[c, d], y1_s.at[c, d], y1_r.at[c, d], y_peers[d])

    def lx_sum(c, d):
        return remote(lxsend.at[c, xs[d]], lxrecv.at[c, d], lx_s.at[c, d], lx_r.at[c, d], x_peers[d])

    def lz_sum(c, d):
        return remote(lzsend.at[c, zs[d]], lzrecv.at[c, d], lz_s.at[c, d], lz_r.at[c, d], z_peers[d])

    def lz_gather(c, d):
        mine = ladder.at[c, x, z]
        return remote(mine, mine, gz_s.at[c, d], gz_r.at[c, d], z_peers[d])

    def lx_gather(c, d):
        mine = ladder.at[c, x]
        return remote(mine, mine, gx_s.at[c, d], gx_r.at[c, d], x_peers[d])

    def by_gather(c, d):
        mine = back.at[c, o]
        return remote(mine, mine, by_s.at[c, d], by_r.at[c, d], y_peers[d])

    def bc_gather(c, d):
        piece = back.at[c, ((y + n_y - d) % n_y) * CORES + core]
        return remote(piece, piece, bc_s.at[c, d], bc_r.at[c, d], core_peer)

    def rx_sum(c, d):
        return remote(rxsend.at[c, xs[d]], rxrecv.at[c, d], rx_s.at[c, d], rx_r.at[c, d], x_peers[d])

    def rz_sum(c, d):
        return remote(rzsend.at[c, zs[d]], rzrecv.at[c, d], rz_s.at[c, d], rz_r.at[c, d], z_peers[d])

    slots = list_ref.shape[1]
    blocks = lax.broadcasted_iota(jnp.int32, (slots, slots), 0)
    places = lax.broadcasted_iota(jnp.int32, (slots, slots), 1)
    live = jnp.logical_and(list_ref[...] == blocks, places < count_ref[...])
    screen = jnp.max(jnp.where(live, 1.0, 0.0), axis=1, keepdims=True)
    for gb in range(GB_DEV):
        for ob in range(OB_DEV):
            number = gb * OB_DEV + ob
            part = (slice(ob * BLK, (ob + 1) * BLK), slice(gb * BLK, (gb + 1) * BLK))
            keep = jnp.broadcast_to(screen[number : number + 1, :], (BLK, BLK))
            masked[part] = (coll_ref[part].astype(F32) * keep).astype(BF16)

    tile = 256
    tiles = pts // tile

    def project(which, dest):
        def step(i, carry):
            q = i // tiles
            at = pl.ds(pl.multiple_of((i % tiles) * tile, tile), tile)
            index = q * CORES + which
            if len(amp_ref.shape) == 3:
                factor = amp_ref[index]
            else:
                factor = amp_ref[:, pl.ds(pl.multiple_of(index * rows_orb, BLK), rows_orb)]
            value = lax.dot_general(
                factor, masked[:, at], (((0,), (0,)), ((), ())), preferred_element_type=F32
            )
            for c in range(chunks):
                for xi in range(n_x):
                    first = xi * rows_dev + c * unit
                    dest[c, q, xi, :, at] = value[first : first + unit]
            return carry

        lax.fori_loop(0, n_y * tiles, step, 0)

    def stage_b(c):
        core_sum(c).wait_recv()
        for d in range(n_y - 1):
            ysend[c, d] = (own1[c, ys[d]] + recv1[c, ys[d]]).astype(BF16)
            y_sum(c, d).start()

    def occ_rows(c):
        return jnp.concatenate(
            [occ_ref[xi * rows_dev + c * unit : xi * rows_dev + (c + 1) * unit, :] for xi in range(n_x)], axis=0
        ).astype(F32)

    def stage_d(c):
        for d in range(n_y - 1):
            y_sum(c, d).wait_recv()
        value = own1[c, y] + recv1[c, y]
        for d in range(n_y - 1):
            value = value + yrecv[c, d].astype(F32)
        had[...] = (value.reshape(wide, pts) * occ_rows(c)).astype(BF16)
        for j in range(n_z):
            value = jnp.dot(had[...], quad_ref[:, j * cols : (j + 1) * cols], preferred_element_type=F32)
            value = value.reshape(n_x, unit, cols)
            lpart[c, :, j] = value
            lxsend[c, :, j] = value.astype(BF16)
        for d in range(n_x - 1):
            lx_sum(c, d).start()

    def stage_e(c):
        for d in range(n_x - 1):
            lx_sum(c, d).wait_recv()
        value = lpart[c, x]
        for d in range(n_x - 1):
            value = value + lxrecv[c, d].astype(F32)
        lzsend[c] = value.astype(BF16)
        for d in range(n_z - 1):
            lz_sum(c, d).start()

    def stage_f(c):
        value = lpart[c, x, z]
        for d in range(n_x - 1):
            value = value + lxrecv[c, d, z].astype(F32)
        for d in range(n_z - 1):
            lz_sum(c, d).wait_recv()
            value = value + lzrecv[c, d].astype(F32)
        ladder[c, x, z] = (value * inv_grid).astype(BF16)
        for d in range(n_z - 1):
            lz_gather(c, d).start()

    def stage_g(c):
        for d in range(n_z - 1):
            lz_gather(c, d).wait_recv()
        for d in range(n_x - 1):
            lx_gather(c, d).start()

    def stage_h(c):
        for d in range(n_x - 1):
            lx_gather(c, d).wait_recv()
        for j in range(n_z):
            ladder_flat[:, j * cols : (j + 1) * cols] = ladder[c, :, j].reshape(wide, cols)
        for i in range(tiles):
            at = slice(i * tile, (i + 1) * tile)
            spread = lax.dot_general(
                ladder_flat[...], quad_ref[at, :], (((1,), (1,)), ((), ())), preferred_element_type=F32
            )
            held = jnp.concatenate(
                [
                    occ_ref[xi * rows_dev + c * unit : xi * rows_dev + (c + 1) * unit, at]
                    for xi in range(n_x)
                ],
                axis=0,
            ).astype(F32)
            back[c, o, :, at] = (held * spread * inv_rank).astype(BF16)
        for d in range(n_y - 1):
            by_gather(c, d).start()
        bc_gather(c, 0).start()

    def stage_i(c):
        for d in range(n_y - 1):
            by_gather(c, d).wait_recv()
            bc_gather(c, d + 1).start()

    def stage_j(c):
        for d in range(n_y):
            bc_gather(c, d).wait_recv()
        def step(i, carry):
            at = pl.ds(pl.multiple_of(i * tile, tile), tile)
            value = lax.dot_general(
                back[c].reshape(n_orb * wide, pts), coll_ref[at, :], (((1,), (1,)), ((), ())),
                preferred_element_type=F32,
            ).reshape(n_orb, n_x, unit, tile)
            for xi in range(n_x):
                rpart[c, xi, :, :, at] = value[:, xi]
                rxsend[c, xi, :, :, at] = value[:, xi].astype(BF16)
            return carry

        lax.fori_loop(0, a_dev // tile, step, 0)
        for d in range(n_x - 1):
            rx_sum(c, d).start()

    def stage_k(c):
        for d in range(n_x - 1):
            rx_sum(c, d).wait_recv()
        value = rpart[c, x]
        for d in range(n_x - 1):
            value = value + rxrecv[c, d].astype(F32)
        rzsend[c] = value.astype(BF16)
        for d in range(n_z - 1):
            rz_sum(c, d).start()

    def stage_l(c):
        value = rpart[c, x, z]
        for d in range(n_x - 1):
            value = value + rxrecv[c, d, z].astype(F32)
        for d in range(n_z - 1):
            rz_sum(c, d).wait_recv()
            value = value + rzrecv[c, d].astype(F32)
        out_ref[c * unit : (c + 1) * unit, :] = value * inv_grid

    project(1 - core, other1)
    pl.semaphore_wait(barrier, len(peers))
    for c in range(chunks):
        core_sum(c).start()
    project(core, own1)

    stages = [stage_b, stage_d, stage_e, stage_f, stage_g, stage_h, stage_i, stage_j, stage_k, stage_l]
    for t in range(len(stages) + chunks - 1):
        for c in range(chunks):
            if 0 <= t - c < len(stages):
                stages[t - c](c)

    for c in range(chunks):
        core_sum(c).wait_send()
        for d in range(n_y - 1):
            y_sum(c, d).wait_send()
            by_gather(c, d).wait_send()
        for d in range(n_y):
            bc_gather(c, d).wait_send()
        for d in range(n_x - 1):
            lx_sum(c, d).wait_send()
            lx_gather(c, d).wait_send()
            rx_sum(c, d).wait_send()
        for d in range(n_z - 1):
            lz_sum(c, d).wait_send()
            lz_gather(c, d).wait_send()
            rz_sum(c, d).wait_send()


def shards(n_grid, n_orb, collocation, amplitude, occupied, quadrature, pair_list, pair_count):
    a_dev, pts = collocation.shape
    rank = amplitude.shape[1]
    n_x = math.isqrt(n_grid // 2)
    n_z = n_grid // n_x
    n_y = n_orb // CORES
    assert n_z == n_orb and n_x * n_z == n_grid
    rows_dev = rank // n_grid
    chunks = rows_dev // UNIT
    wide = n_x * UNIT
    cols = rank // n_z
    if (rank // n_orb) % BLK:
        amplitude = amplitude.reshape(a_dev, n_orb, rank // n_orb).transpose(1, 0, 2)
    vmem = pltpu.VMEM

    def sems(n):
        return [pltpu.SemaphoreType.DMA((chunks, n))] * 2

    one = [pltpu.SemaphoreType.DMA((chunks,))] * 2
    return pl.pallas_call(
        functools.partial(kernel, n_grid, n_orb, n_x, chunks, pts * n_grid),
        out_shape=jax.ShapeDtypeStruct((rows_dev, a_dev), F32),
        in_specs=[pl.BlockSpec(memory_space=vmem)] * 6,
        out_specs=pl.BlockSpec(memory_space=vmem),
        scratch_shapes=[
            vmem((a_dev, pts), BF16),
            vmem((chunks, n_y, n_x, UNIT, pts), F32),
            vmem((chunks, n_y, n_x, UNIT, pts), F32),
            vmem((chunks, n_y, n_x, UNIT, pts), F32),
            vmem((chunks, n_y - 1, n_x, UNIT, pts), BF16),
            vmem((chunks, n_y - 1, n_x, UNIT, pts), BF16),
            vmem((wide, pts), BF16),
            vmem((chunks, n_x, n_z, UNIT, cols), F32),
            vmem((chunks, n_x, n_z, UNIT, cols), BF16),
            vmem((chunks, n_x - 1, n_z, UNIT, cols), BF16),
            vmem((chunks, n_z, UNIT, cols), BF16),
            vmem((chunks, n_z - 1, UNIT, cols), BF16),
            vmem((chunks, n_x, n_z, UNIT, cols), BF16),
            vmem((wide, rank), BF16),
            vmem((chunks, n_orb, wide, pts), BF16),
            vmem((chunks, n_x, n_orb, UNIT, a_dev), F32),
            vmem((chunks, n_x, n_orb, UNIT, a_dev), BF16),
            vmem((chunks, n_x - 1, n_orb, UNIT, a_dev), BF16),
            vmem((chunks, n_orb, UNIT, a_dev), BF16),
            vmem((chunks, n_z - 1, UNIT, a_dev), BF16),
            *one,
            *sems(n_y - 1),
            *sems(n_x - 1),
            *sems(n_z - 1),
            *sems(n_z - 1),
            *sems(n_x - 1),
            *sems(n_y - 1),
            *sems(n_y),
            *sems(n_x - 1),
            *sems(n_z - 1),
        ],
        compiler_params=pltpu.CompilerParams(
            collective_id=0, has_side_effects=True, vmem_limit_bytes=60 * 2**20
        ),
        cost_estimate=pl.CostEstimate(
            flops=2 * a_dev * rank * pts * 2 + 4 * (rank // n_orb) * pts * rank,
            bytes_accessed=10_000_000,
            transcendentals=0,
        ),
    )(
        collocation, amplitude, occupied, quadrature,
        pair_list.reshape(1, -1), pair_count.reshape(1, 1),
    )


def solution(mesh):
    return jax.shard_map(
        functools.partial(shards, mesh.shape["grid"], mesh.shape["orb"]),
        mesh=mesh,
        in_specs=(
            P("orb", "grid"),
            P("orb", None),
            P("orb", "grid"),
            P("grid", None),
            P("grid", "orb", None),
            P("grid", "orb"),
        ),
        out_specs=P("grid", "orb"),
        check_vma=False,
    )
```

```python
import functools
import math

import jax
import jax.numpy as jnp
from jax import lax
from jax.experimental import pallas as pl
from jax.experimental.pallas import tpu as pltpu
from jax.sharding import PartitionSpec as P

BLK = 128
OB_DEV = 6
GB_DEV = 8
CORES = 2
UNIT = 48
MESH = pl.DeviceIdType.MESH
F32 = jnp.float32
BF16 = jnp.bfloat16


def kernel(
    n_grid, n_orb, n_x, chunks, total_grid,
    coll_ref, amp_ref, occ_hbm, quad_hbm, list_ref, count_ref, out_ref,
    occ_ref, quad_ref, load_sem,
    masked, other1, own1, recv1, ysend, yrecv, had, lpart, lxsend, lxrecv, lzsend, lzrecv,
    ladder, ladder_flat, back, rpart, rxsend, rxrecv, rzsend, rzrecv,
    c1_s, c1_r, y1_s, y1_r, lx_s, lx_r, lz_s, lz_r, gz_s, gz_r, gx_s, gx_r,
    by_s, by_r, bc_s, bc_r, rx_s, rx_r, rz_s, rz_r,
):
    n_y = n_orb // CORES
    n_z = n_grid // n_x
    a_dev, pts = coll_ref.shape
    rank = quad_hbm.shape[1]
    rows_orb = rank // n_orb
    rows_dev = rank // n_grid
    unit = rows_dev // chunks
    wide = n_x * unit
    cols = rank // n_z
    inv_grid = 1.0 / math.sqrt(total_grid)
    inv_rank = 1.0 / math.sqrt(rank)

    g, o = lax.axis_index("grid"), lax.axis_index("orb")
    z, x = g // n_x, g % n_x
    y, core = o // CORES, o % CORES

    core_peer = (g, y * CORES + (1 - core))
    ys = [(y + d) % n_y for d in range(1, n_y)]
    xs = [(x + d) % n_x for d in range(1, n_x)]
    zs = [(z + d) % n_z for d in range(1, n_z)]
    y_peers = [(g, q * CORES + core) for q in ys]
    x_peers = [(z * n_x + q, o) for q in xs]
    z_peers = [(q * n_x + x, o) for q in zs]

    barrier = pltpu.get_barrier_semaphore()
    peers = [core_peer] + y_peers + x_peers + z_peers
    for peer in peers:
        pl.semaphore_signal(barrier, inc=1, device_id=peer, device_id_type=MESH)

    def remote(src, dst, send, recv, peer):
        return pltpu.make_async_remote_copy(
            src_ref=src, dst_ref=dst, send_sem=send, recv_sem=recv, device_id=peer, device_id_type=MESH
        )

    def core_sum(c):
        return remote(other1.at[c], recv1.at[c], c1_s.at[c], c1_r.at[c], core_peer)

    def y_sum(c, d):
        return remote(ysend.at[c, d], yrecv.at[c, d], y1_s.at[c, d], y1_r.at[c, d], y_peers[d])

    def lx_sum(c, d):
        return remote(lxsend.at[c, xs[d]], lxrecv.at[c, d], lx_s.at[c, d], lx_r.at[c, d], x_peers[d])

    def lz_sum(c, d):
        return remote(lzsend.at[c, zs[d]], lzrecv.at[c, d], lz_s.at[c, d], lz_r.at[c, d], z_peers[d])

    def lz_gather(c, d):
        mine = ladder.at[c, x, z]
        return remote(mine, mine, gz_s.at[c, d], gz_r.at[c, d], z_peers[d])

    def lx_gather(c, d):
        mine = ladder.at[c, x]
        return remote(mine, mine, gx_s.at[c, d], gx_r.at[c, d], x_peers[d])

    def by_gather(c, d):
        mine = back.at[c, o]
        return remote(mine, mine, by_s.at[c, d], by_r.at[c, d], y_peers[d])

    def bc_gather(c, d):
        piece = back.at[c, ((y + n_y - d) % n_y) * CORES + core]
        return remote(piece, piece, bc_s.at[c, d], bc_r.at[c, d], core_peer)

    def rx_sum(c, d):
        return remote(rxsend.at[c, xs[d]], rxrecv.at[c, d], rx_s.at[c, d], rx_r.at[c, d], x_peers[d])

    def rz_sum(c, d):
        return remote(rzsend.at[c, zs[d]], rzrecv.at[c, d], rz_s.at[c, d], rz_r.at[c, d], z_peers[d])

    loads = [
        pltpu.make_async_copy(occ_hbm, occ_ref, load_sem.at[0]),
        pltpu.make_async_copy(quad_hbm, quad_ref, load_sem.at[1]),
    ]
    for load in loads:
        load.start()

    slots = list_ref.shape[1]
    blocks = lax.broadcasted_iota(jnp.int32, (slots, slots), 0)
    places = lax.broadcasted_iota(jnp.int32, (slots, slots), 1)
    live = jnp.logical_and(list_ref[...] == blocks, places < count_ref[...])
    screen = jnp.max(jnp.where(live, 1.0, 0.0), axis=1, keepdims=True)
    for gb in range(GB_DEV):
        for ob in range(OB_DEV):
            number = gb * OB_DEV + ob
            part = (slice(ob * BLK, (ob + 1) * BLK), slice(gb * BLK, (gb + 1) * BLK))
            keep = jnp.broadcast_to(screen[number : number + 1, :], (BLK, BLK))
            masked[part] = (coll_ref[part].astype(F32) * keep).astype(BF16)

    tile = 256
    tiles = pts // tile

    def project(which, dest):
        def step(i, carry):
            q = i // tiles
            at = pl.ds(pl.multiple_of((i % tiles) * tile, tile), tile)
            index = q * CORES + which
            if len(amp_ref.shape) == 3:
                factor = amp_ref[index]
            else:
                factor = amp_ref[:, pl.ds(pl.multiple_of(index * rows_orb, BLK), rows_orb)]
            value = lax.dot_general(
                factor, masked[:, at], (((0,), (0,)), ((), ())), preferred_element_type=F32
            )
            for c in range(chunks):
                for xi in range(n_x):
                    first = xi * rows_dev + c * unit
                    dest[c, q, xi, :, at] = value[first : first + unit]
            return carry

        lax.fori_loop(0, n_y * tiles, step, 0)

    def stage_b(c):
        core_sum(c).wait_recv()
        for d in range(n_y - 1):
            ysend[c, d] = (own1[c, ys[d]] + recv1[c, ys[d]]).astype(BF16)
            y_sum(c, d).start()

    def occ_rows(c):
        return jnp.concatenate(
            [occ_ref[xi * rows_dev + c * unit : xi * rows_dev + (c + 1) * unit, :] for xi in range(n_x)], axis=0
        ).astype(F32)

    def stage_d(c):
        for d in range(n_y - 1):
            y_sum(c, d).wait_recv()
        value = own1[c, y] + recv1[c, y]
        for d in range(n_y - 1):
            value = value + yrecv[c, d].astype(F32)
        had[...] = (value.reshape(wide, pts) * occ_rows(c)).astype(BF16)
        for j in range(n_z):
            value = jnp.dot(had[...], quad_ref[:, j * cols : (j + 1) * cols], preferred_element_type=F32)
            value = value.reshape(n_x, unit, cols)
            lpart[c, :, j] = value
            lxsend[c, :, j] = value.astype(BF16)
        for d in range(n_x - 1):
            lx_sum(c, d).start()

    def stage_e(c):
        for d in range(n_x - 1):
            lx_sum(c, d).wait_recv()
        value = lpart[c, x]
        for d in range(n_x - 1):
            value = value + lxrecv[c, d].astype(F32)
        lzsend[c] = value.astype(BF16)
        for d in range(n_z - 1):
            lz_sum(c, d).start()

    def stage_f(c):
        value = lpart[c, x, z]
        for d in range(n_x - 1):
            value = value + lxrecv[c, d, z].astype(F32)
        for d in range(n_z - 1):
            lz_sum(c, d).wait_recv()
            value = value + lzrecv[c, d].astype(F32)
        ladder[c, x, z] = (value * inv_grid).astype(BF16)
        for d in range(n_z - 1):
            lz_gather(c, d).start()

    def stage_g(c):
        for d in range(n_z - 1):
            lz_gather(c, d).wait_recv()
        for d in range(n_x - 1):
            lx_gather(c, d).start()

    def stage_h(c):
        for d in range(n_x - 1):
            lx_gather(c, d).wait_recv()
        for j in range(n_z):
            ladder_flat[:, j * cols : (j + 1) * cols] = ladder[c, :, j].reshape(wide, cols)
        for i in range(tiles):
            at = slice(i * tile, (i + 1) * tile)
            spread = lax.dot_general(
                ladder_flat[...], quad_ref[at, :], (((1,), (1,)), ((), ())), preferred_element_type=F32
            )
            held = jnp.concatenate(
                [
                    occ_ref[xi * rows_dev + c * unit : xi * rows_dev + (c + 1) * unit, at]
                    for xi in range(n_x)
                ],
                axis=0,
            ).astype(F32)
            back[c, o, :, at] = (held * spread * inv_rank).astype(BF16)
        for d in range(n_y - 1):
            by_gather(c, d).start()
        bc_gather(c, 0).start()

    def stage_i(c):
        for d in range(n_y - 1):
            by_gather(c, d).wait_recv()
            bc_gather(c, d + 1).start()

    def stage_j(c):
        for d in range(n_y):
            bc_gather(c, d).wait_recv()
        def step(i, carry):
            at = pl.ds(pl.multiple_of(i * tile, tile), tile)
            value = lax.dot_general(
                back[c].reshape(n_orb * wide, pts), coll_ref[at, :], (((1,), (1,)), ((), ())),
                preferred_element_type=F32,
            ).reshape(n_orb, n_x, unit, tile)
            for xi in range(n_x):
                rpart[c, xi, :, :, at] = value[:, xi]
                rxsend[c, xi, :, :, at] = value[:, xi].astype(BF16)
            return carry

        lax.fori_loop(0, a_dev // tile, step, 0)
        for d in range(n_x - 1):
            rx_sum(c, d).start()

    def stage_k(c):
        for d in range(n_x - 1):
            rx_sum(c, d).wait_recv()
        value = rpart[c, x]
        for d in range(n_x - 1):
            value = value + rxrecv[c, d].astype(F32)
        rzsend[c] = value.astype(BF16)
        for d in range(n_z - 1):
            rz_sum(c, d).start()

    def stage_l(c):
        value = rpart[c, x, z]
        for d in range(n_x - 1):
            value = value + rxrecv[c, d, z].astype(F32)
        for d in range(n_z - 1):
            rz_sum(c, d).wait_recv()
            value = value + rzrecv[c, d].astype(F32)
        out_ref[c * unit : (c + 1) * unit, :] = value * inv_grid

    project(1 - core, other1)
    pl.semaphore_wait(barrier, len(peers))
    for c in range(chunks):
        core_sum(c).start()
    project(core, own1)
    for load in loads:
        load.wait()

    stages = [stage_b, stage_d, stage_e, stage_f, stage_g, stage_h, stage_i, stage_j, stage_k, stage_l]
    for t in range(len(stages) + chunks - 1):
        for c in range(chunks):
            if 0 <= t - c < len(stages):
                stages[t - c](c)

    for c in range(chunks):
        core_sum(c).wait_send()
        for d in range(n_y - 1):
            y_sum(c, d).wait_send()
            by_gather(c, d).wait_send()
        for d in range(n_y):
            bc_gather(c, d).wait_send()
        for d in range(n_x - 1):
            lx_sum(c, d).wait_send()
            lx_gather(c, d).wait_send()
            rx_sum(c, d).wait_send()
        for d in range(n_z - 1):
            lz_sum(c, d).wait_send()
            lz_gather(c, d).wait_send()
            rz_sum(c, d).wait_send()


def shards(n_grid, n_orb, collocation, amplitude, occupied, quadrature, pair_list, pair_count):
    a_dev, pts = collocation.shape
    rank = amplitude.shape[1]
    n_x = math.isqrt(n_grid // 2)
    n_z = n_grid // n_x
    n_y = n_orb // CORES
    assert n_z == n_orb and n_x * n_z == n_grid
    rows_dev = rank // n_grid
    chunks = rows_dev // UNIT
    wide = n_x * UNIT
    cols = rank // n_z
    if (rank // n_orb) % BLK:
        amplitude = amplitude.reshape(a_dev, n_orb, rank // n_orb).transpose(1, 0, 2)
    vmem = pltpu.VMEM

    def sems(n):
        return [pltpu.SemaphoreType.DMA((chunks, n))] * 2

    one = [pltpu.SemaphoreType.DMA((chunks,))] * 2
    return pl.pallas_call(
        functools.partial(kernel, n_grid, n_orb, n_x, chunks, pts * n_grid),
        out_shape=jax.ShapeDtypeStruct((rows_dev, a_dev), F32),
        in_specs=[pl.BlockSpec(memory_space=m) for m in (vmem, vmem, pl.ANY, pl.ANY, vmem, vmem)],
        out_specs=pl.BlockSpec(memory_space=vmem),
        scratch_shapes=[
            vmem(occupied.shape, BF16),
            vmem(quadrature.shape, BF16),
            pltpu.SemaphoreType.DMA((2,)),
            vmem((a_dev, pts), BF16),
            vmem((chunks, n_y, n_x, UNIT, pts), F32),
            vmem((chunks, n_y, n_x, UNIT, pts), F32),
            vmem((chunks, n_y, n_x, UNIT, pts), F32),
            vmem((chunks, n_y - 1, n_x, UNIT, pts), BF16),
            vmem((chunks, n_y - 1, n_x, UNIT, pts), BF16),
            vmem((wide, pts), BF16),
            vmem((chunks, n_x, n_z, UNIT, cols), F32),
            vmem((chunks, n_x, n_z, UNIT, cols), BF16),
            vmem((chunks, n_x - 1, n_z, UNIT, cols), BF16),
            vmem((chunks, n_z, UNIT, cols), BF16),
            vmem((chunks, n_z - 1, UNIT, cols), BF16),
            vmem((chunks, n_x, n_z, UNIT, cols), BF16),
            vmem((wide, rank), BF16),
            vmem((chunks, n_orb, wide, pts), BF16),
            vmem((chunks, n_x, n_orb, UNIT, a_dev), F32),
            vmem((chunks, n_x, n_orb, UNIT, a_dev), BF16),
            vmem((chunks, n_x - 1, n_orb, UNIT, a_dev), BF16),
            vmem((chunks, n_orb, UNIT, a_dev), BF16),
            vmem((chunks, n_z - 1, UNIT, a_dev), BF16),
            *one,
            *sems(n_y - 1),
            *sems(n_x - 1),
            *sems(n_z - 1),
            *sems(n_z - 1),
            *sems(n_x - 1),
            *sems(n_y - 1),
            *sems(n_y),
            *sems(n_x - 1),
            *sems(n_z - 1),
        ],
        compiler_params=pltpu.CompilerParams(
            collective_id=0, has_side_effects=True, vmem_limit_bytes=60 * 2**20
        ),
        cost_estimate=pl.CostEstimate(
            flops=2 * a_dev * rank * pts * 2 + 4 * (rank // n_orb) * pts * rank,
            bytes_accessed=10_000_000,
            transcendentals=0,
        ),
    )(
        collocation, amplitude, occupied, quadrature,
        pair_list.reshape(1, -1), pair_count.reshape(1, 1),
    )


def solution(mesh):
    return jax.shard_map(
        functools.partial(shards, mesh.shape["grid"], mesh.shape["orb"]),
        mesh=mesh,
        in_specs=(
            P("orb", "grid"),
            P("orb", None),
            P("orb", "grid"),
            P("grid", None),
            P("grid", "orb", None),
            P("grid", "orb"),
        ),
        out_specs=P("grid", "orb"),
        check_vma=False,
    )
```

```python
import functools
import math

import jax
import jax.numpy as jnp
from jax import lax
from jax.experimental import pallas as pl
from jax.experimental.pallas import tpu as pltpu
from jax.sharding import PartitionSpec as P

BLK = 128
OB_DEV = 6
GB_DEV = 8
CORES = 2
UNIT = 48
MESH = pl.DeviceIdType.MESH
F32 = jnp.float32
BF16 = jnp.bfloat16


def kernel(
    n_grid, n_orb, n_x, chunks, total_grid,
    coll_ref, amp_ref, occ_hbm, quad_hbm, list_ref, count_ref, out_ref,
    occ_ref, quad_ref, load_sem,
    masked, other1, own1, recv1, ysend, yrecv, had, lpart, lxsend, lxrecv, lzsend, lzrecv,
    ladder, ladder_flat, back, rpart, rxsend, rxrecv, rzsend, rzrecv,
    c1_s, c1_r, y1_s, y1_r, lx_s, lx_r, lz_s, lz_r, gz_s, gz_r, gx_s, gx_r,
    by_s, by_r, bc_s, bc_r, rx_s, rx_r, rz_s, rz_r,
):
    n_y = n_orb // CORES
    n_z = n_grid // n_x
    a_dev, pts = coll_ref.shape
    rank = quad_hbm.shape[1]
    rows_orb = rank // n_orb
    rows_dev = rank // n_grid
    unit = rows_dev // chunks
    wide = n_x * unit
    cols = rank // n_z
    inv_grid = 1.0 / math.sqrt(total_grid)
    inv_rank = 1.0 / math.sqrt(rank)

    g, o = lax.axis_index("grid"), lax.axis_index("orb")
    z, x = g // n_x, g % n_x
    y, core = o // CORES, o % CORES

    core_peer = (g, y * CORES + (1 - core))
    ys = [(y + d) % n_y for d in range(1, n_y)]
    xs = [(x + d) % n_x for d in range(1, n_x)]
    zs = [(z + d) % n_z for d in range(1, n_z)]
    y_peers = [(g, q * CORES + core) for q in ys]
    x_peers = [(z * n_x + q, o) for q in xs]
    z_peers = [(q * n_x + x, o) for q in zs]

    barrier = pltpu.get_barrier_semaphore()
    peers = [core_peer] + y_peers + x_peers + z_peers
    for peer in peers:
        pl.semaphore_signal(barrier, inc=1, device_id=peer, device_id_type=MESH)

    def remote(src, dst, send, recv, peer):
        return pltpu.make_async_remote_copy(
            src_ref=src, dst_ref=dst, send_sem=send, recv_sem=recv, device_id=peer, device_id_type=MESH
        )

    def core_sum(c, d):
        q = (y + 1 + d) % n_y
        return remote(other1.at[c, q], recv1.at[c, q], c1_s.at[c, d], c1_r.at[c, d], core_peer)

    def y_sum(c, d):
        return remote(ysend.at[c, d], yrecv.at[c, d], y1_s.at[c, d], y1_r.at[c, d], y_peers[d])

    def lx_sum(c, d):
        return remote(lxsend.at[c, xs[d]], lxrecv.at[c, d], lx_s.at[c, d], lx_r.at[c, d], x_peers[d])

    def lz_sum(c, d):
        return remote(lzsend.at[c, zs[d]], lzrecv.at[c, d], lz_s.at[c, d], lz_r.at[c, d], z_peers[d])

    def lz_gather(c, d):
        mine = ladder.at[c, x, z]
        return remote(mine, mine, gz_s.at[c, d], gz_r.at[c, d], z_peers[d])

    def lx_gather(c, d):
        mine = ladder.at[c, x]
        return remote(mine, mine, gx_s.at[c, d], gx_r.at[c, d], x_peers[d])

    def by_gather(c, d):
        mine = back.at[c, o]
        return remote(mine, mine, by_s.at[c, d], by_r.at[c, d], y_peers[d])

    def bc_gather(c, d):
        piece = back.at[c, ((y + n_y - d) % n_y) * CORES + core]
        return remote(piece, piece, bc_s.at[c, d], bc_r.at[c, d], core_peer)

    def rx_sum(c, d):
        return remote(rxsend.at[c, xs[d]], rxrecv.at[c, d], rx_s.at[c, d], rx_r.at[c, d], x_peers[d])

    def rz_sum(c, d):
        return remote(rzsend.at[c, zs[d]], rzrecv.at[c, d], rz_s.at[c, d], rz_r.at[c, d], z_peers[d])

    loads = [
        pltpu.make_async_copy(occ_hbm, occ_ref, load_sem.at[0]),
        pltpu.make_async_copy(quad_hbm, quad_ref, load_sem.at[1]),
    ]
    for load in loads:
        load.start()

    slots = list_ref.shape[1]
    blocks = lax.broadcasted_iota(jnp.int32, (slots, slots), 0)
    places = lax.broadcasted_iota(jnp.int32, (slots, slots), 1)
    live = jnp.logical_and(list_ref[...] == blocks, places < count_ref[...])
    screen = jnp.max(jnp.where(live, 1.0, 0.0), axis=1, keepdims=True)
    for gb in range(GB_DEV):
        for ob in range(OB_DEV):
            number = gb * OB_DEV + ob
            part = (slice(ob * BLK, (ob + 1) * BLK), slice(gb * BLK, (gb + 1) * BLK))
            keep = jnp.broadcast_to(screen[number : number + 1, :], (BLK, BLK))
            masked[part] = (coll_ref[part].astype(F32) * keep).astype(BF16)

    tile = 256
    tiles = pts // tile

    def project(which, dest, first_block, last_block):
        def step(i, carry):
            q = (y + 1 + i // tiles) % n_y
            at = pl.ds(pl.multiple_of((i % tiles) * tile, tile), tile)
            index = q * CORES + which
            if len(amp_ref.shape) == 3:
                factor = amp_ref[index]
            else:
                factor = amp_ref[:, pl.ds(pl.multiple_of(index * rows_orb, BLK), rows_orb)]
            value = lax.dot_general(
                factor, masked[:, at], (((0,), (0,)), ((), ())), preferred_element_type=F32
            )
            for c in range(chunks):
                for xi in range(n_x):
                    first = xi * rows_dev + c * unit
                    dest[c, q, xi, :, at] = value[first : first + unit]
            return carry

        lax.fori_loop(first_block * tiles, last_block * tiles, step, 0)

    def stage_b(c):
        for d in range(n_y - 1):
            core_sum(c, d).wait_recv()
            ysend[c, d] = (own1[c, ys[d]] + recv1[c, ys[d]]).astype(BF16)
            y_sum(c, d).start()

    def occ_rows(c):
        return jnp.concatenate(
            [occ_ref[xi * rows_dev + c * unit : xi * rows_dev + (c + 1) * unit, :] for xi in range(n_x)], axis=0
        ).astype(F32)

    def stage_d(c):
        for d in range(n_y - 1):
            y_sum(c, d).wait_recv()
        core_sum(c, n_y - 1).wait_recv()
        value = own1[c, y] + recv1[c, y]
        for d in range(n_y - 1):
            value = value + yrecv[c, d].astype(F32)
        had[...] = (value.reshape(wide, pts) * occ_rows(c)).astype(BF16)
        for j in range(n_z):
            value = jnp.dot(had[...], quad_ref[:, j * cols : (j + 1) * cols], preferred_element_type=F32)
            value = value.reshape(n_x, unit, cols)
            lpart[c, :, j] = value
            lxsend[c, :, j] = value.astype(BF16)
        for d in range(n_x - 1):
            lx_sum(c, d).start()

    def stage_e(c):
        for d in range(n_x - 1):
            lx_sum(c, d).wait_recv()
        value = lpart[c, x]
        for d in range(n_x - 1):
            value = value + lxrecv[c, d].astype(F32)
        lzsend[c] = value.astype(BF16)
        for d in range(n_z - 1):
            lz_sum(c, d).start()

    def stage_f(c):
        value = lpart[c, x, z]
        for d in range(n_x - 1):
            value = value + lxrecv[c, d, z].astype(F32)
        for d in range(n_z - 1):
            lz_sum(c, d).wait_recv()
            value = value + lzrecv[c, d].astype(F32)
        ladder[c, x, z] = (value * inv_grid).astype(BF16)
        for d in range(n_z - 1):
            lz_gather(c, d).start()

    def stage_g(c):
        for d in range(n_z - 1):
            lz_gather(c, d).wait_recv()
        for d in range(n_x - 1):
            lx_gather(c, d).start()

    def stage_h(c):
        for d in range(n_x - 1):
            lx_gather(c, d).wait_recv()
        for j in range(n_z):
            ladder_flat[:, j * cols : (j + 1) * cols] = ladder[c, :, j].reshape(wide, cols)
        for i in range(tiles):
            at = slice(i * tile, (i + 1) * tile)
            spread = lax.dot_general(
                ladder_flat[...], quad_ref[at, :], (((1,), (1,)), ((), ())), preferred_element_type=F32
            )
            held = jnp.concatenate(
                [
                    occ_ref[xi * rows_dev + c * unit : xi * rows_dev + (c + 1) * unit, at]
                    for xi in range(n_x)
                ],
                axis=0,
            ).astype(F32)
            back[c, o, :, at] = (held * spread * inv_rank).astype(BF16)
        for d in range(n_y - 1):
            by_gather(c, d).start()
        bc_gather(c, 0).start()

    def stage_i(c):
        for d in range(n_y - 1):
            by_gather(c, d).wait_recv()
            bc_gather(c, d + 1).start()

    def stage_j(c):
        for d in range(n_y):
            bc_gather(c, d).wait_recv()
        def step(i, carry):
            at = pl.ds(pl.multiple_of(i * tile, tile), tile)
            value = lax.dot_general(
                back[c].reshape(n_orb * wide, pts), coll_ref[at, :], (((1,), (1,)), ((), ())),
                preferred_element_type=F32,
            ).reshape(n_orb, n_x, unit, tile)
            for xi in range(n_x):
                rpart[c, xi, :, :, at] = value[:, xi]
                rxsend[c, xi, :, :, at] = value[:, xi].astype(BF16)
            return carry

        lax.fori_loop(0, a_dev // tile, step, 0)
        for d in range(n_x - 1):
            rx_sum(c, d).start()

    def stage_k(c):
        for d in range(n_x - 1):
            rx_sum(c, d).wait_recv()
        value = rpart[c, x]
        for d in range(n_x - 1):
            value = value + rxrecv[c, d].astype(F32)
        rzsend[c] = value.astype(BF16)
        for d in range(n_z - 1):
            rz_sum(c, d).start()

    def stage_l(c):
        value = rpart[c, x, z]
        for d in range(n_x - 1):
            value = value + rxrecv[c, d, z].astype(F32)
        for d in range(n_z - 1):
            rz_sum(c, d).wait_recv()
            value = value + rzrecv[c, d].astype(F32)
        out_ref[c * unit : (c + 1) * unit, :] = value * inv_grid

    project(1 - core, other1, 0, n_y - 1)
    pl.semaphore_wait(barrier, len(peers))
    for c in range(chunks):
        for d in range(n_y - 1):
            core_sum(c, d).start()
    project(core, own1, 0, n_y - 1)
    for c in range(chunks):
        stage_b(c)
    project(1 - core, other1, n_y - 1, n_y)
    for c in range(chunks):
        core_sum(c, n_y - 1).start()
    project(core, own1, n_y - 1, n_y)
    for load in loads:
        load.wait()

    stages = [stage_d, stage_e, stage_f, stage_g, stage_h, stage_i, stage_j, stage_k, stage_l]
    times = (2, 4, 6, 7, 9, 11, 12, 14, 16)
    order = sorted((times[s] + 2 * c, c, s) for s in range(len(stages)) for c in range(chunks))
    for _, c, s in order:
        stages[s](c)

    for c in range(chunks):
        for d in range(n_y):
            core_sum(c, d).wait_send()
        for d in range(n_y - 1):
            y_sum(c, d).wait_send()
            by_gather(c, d).wait_send()
        for d in range(n_y):
            bc_gather(c, d).wait_send()
        for d in range(n_x - 1):
            lx_sum(c, d).wait_send()
            lx_gather(c, d).wait_send()
            rx_sum(c, d).wait_send()
        for d in range(n_z - 1):
            lz_sum(c, d).wait_send()
            lz_gather(c, d).wait_send()
            rz_sum(c, d).wait_send()


def shards(n_grid, n_orb, collocation, amplitude, occupied, quadrature, pair_list, pair_count):
    a_dev, pts = collocation.shape
    rank = amplitude.shape[1]
    n_x = math.isqrt(n_grid // 2)
    n_z = n_grid // n_x
    n_y = n_orb // CORES
    assert n_z == n_orb and n_x * n_z == n_grid
    rows_dev = rank // n_grid
    chunks = rows_dev // UNIT
    wide = n_x * UNIT
    cols = rank // n_z
    if (rank // n_orb) % BLK:
        amplitude = amplitude.reshape(a_dev, n_orb, rank // n_orb).transpose(1, 0, 2)
    vmem = pltpu.VMEM

    def sems(n):
        return [pltpu.SemaphoreType.DMA((chunks, n))] * 2

    return pl.pallas_call(
        functools.partial(kernel, n_grid, n_orb, n_x, chunks, pts * n_grid),
        out_shape=jax.ShapeDtypeStruct((rows_dev, a_dev), F32),
        in_specs=[pl.BlockSpec(memory_space=m) for m in (vmem, vmem, pl.ANY, pl.ANY, vmem, vmem)],
        out_specs=pl.BlockSpec(memory_space=vmem),
        scratch_shapes=[
            vmem(occupied.shape, BF16),
            vmem(quadrature.shape, BF16),
            pltpu.SemaphoreType.DMA((2,)),
            vmem((a_dev, pts), BF16),
            vmem((chunks, n_y, n_x, UNIT, pts), F32),
            vmem((chunks, n_y, n_x, UNIT, pts), F32),
            vmem((chunks, n_y, n_x, UNIT, pts), F32),
            vmem((chunks, n_y - 1, n_x, UNIT, pts), BF16),
            vmem((chunks, n_y - 1, n_x, UNIT, pts), BF16),
            vmem((wide, pts), BF16),
            vmem((chunks, n_x, n_z, UNIT, cols), F32),
            vmem((chunks, n_x, n_z, UNIT, cols), BF16),
            vmem((chunks, n_x - 1, n_z, UNIT, cols), BF16),
            vmem((chunks, n_z, UNIT, cols), BF16),
            vmem((chunks, n_z - 1, UNIT, cols), BF16),
            vmem((chunks, n_x, n_z, UNIT, cols), BF16),
            vmem((wide, rank), BF16),
            vmem((chunks, n_orb, wide, pts), BF16),
            vmem((chunks, n_x, n_orb, UNIT, a_dev), F32),
            vmem((chunks, n_x, n_orb, UNIT, a_dev), BF16),
            vmem((chunks, n_x - 1, n_orb, UNIT, a_dev), BF16),
            vmem((chunks, n_orb, UNIT, a_dev), BF16),
            vmem((chunks, n_z - 1, UNIT, a_dev), BF16),
            *sems(n_y),
            *sems(n_y - 1),
            *sems(n_x - 1),
            *sems(n_z - 1),
            *sems(n_z - 1),
            *sems(n_x - 1),
            *sems(n_y - 1),
            *sems(n_y),
            *sems(n_x - 1),
            *sems(n_z - 1),
        ],
        compiler_params=pltpu.CompilerParams(
            collective_id=0, has_side_effects=True, vmem_limit_bytes=60 * 2**20
        ),
        cost_estimate=pl.CostEstimate(
            flops=2 * a_dev * rank * pts * 2 + 4 * (rank // n_orb) * pts * rank,
            bytes_accessed=10_000_000,
            transcendentals=0,
        ),
    )(
        collocation, amplitude, occupied, quadrature,
        pair_list.reshape(1, -1), pair_count.reshape(1, 1),
    )


def solution(mesh):
    return jax.shard_map(
        functools.partial(shards, mesh.shape["grid"], mesh.shape["orb"]),
        mesh=mesh,
        in_specs=(
            P("orb", "grid"),
            P("orb", None),
            P("orb", "grid"),
            P("grid", None),
            P("grid", "orb", None),
            P("grid", "orb"),
        ),
        out_specs=P("grid", "orb"),
        check_vma=False,
    )
```
